32 devices in a mesh: wide: 8 (over z, x), lend: 4 (over y, core).
Axes of the slice: x: 2, y: 2, z: 4, core: 2. Of those that a mesh axis runs over, the one named last changes fastest.
Arguments:
- operators: bfloat16 [4, 8, 1024, 1024], P('lend', 'wide'), as said below
- dual_rhs: float32 [4, 4096, 128], P('lend', 'wide'), may hold values from -6 to 6
- contact: int32 [4, 4096], P('lend', 'wide'), may hold values 0 or 1
- costs: int32 [4, 8], P('lend', 'wide'), may hold values from 1 to 8, as said below
Outputs:
- multipliers: float32 [4, 4096, 128], P('lend', 'wide')
- gradient: float32 [4, 4096, 128], P('lend', 'wide')
The draws below stay inside these ranges and needn't reach their ends.
Inputs may be any that keep to these rules, and one draw needn't show every extreme that they name: `operators`: each subdomain's operator is symmetric positive definite up to rounding. 1 marks a contact multiplier that must stay nonnegative, 0 a gluing one. The number of live blocks of 128 slots of each subdomain; its live slots are the first costs * 128. For every j, costs[2 j, w] + costs[2 j + 1, w] is at most 9.
All inputs are finite; a program needn't handle non-finite values. No bound on the sum of `contact` on one device may be relied on, other than what follows from the above.
Results may differ from the reference program's by a relative error of at most 0.0086.
Values may be sent and summed in bfloat16 or wider, within the bound.
A program may use at most 64 MiB of HBM per device.

```python
import jax
import jax.numpy as jnp
from jax import lax

M = 1024
ROWBLK = 128
K = 128
ITERS = 4
FACE = 512
MULTS = 4096
N_WIDE = 8
N_LEND = 4


def draw_operators(key, part):

    def single(number):
        subkey = jax.random.fold_in(key, number)
        first_key, second_key = jax.random.split(subkey, 2)
        gaussian = jax.random.normal(first_key, (M, M), jnp.float32)
        coupling = (gaussian + gaussian.T) * (0.5 / jnp.sqrt(2.0 * M))
        diagonal_part = jax.random.uniform(second_key, (M,), jnp.float32, 1.5, 3.0)
        matrix = coupling + jnp.diag(diagonal_part)
        return matrix.astype(jnp.bfloat16)
    stacked = lax.map(single, jnp.arange(N_LEND * N_WIDE, dtype=jnp.int32))
    return stacked.reshape(N_LEND, N_WIDE, M, M)


def draw_costs(key, part):
    most = M // ROWBLK
    base_key = jax.random.fold_in(key, 7301)
    first_key, second_key, third_key = jax.random.split(base_key, 3)
    shape = (N_LEND // 2, N_WIDE)
    heavy = jax.random.randint(first_key, shape, 1, most + 1, dtype=jnp.int32)
    heavy = heavy.at[0, 0].set(most)
    light = jax.random.randint(second_key, shape, 1, most + 2 - heavy, dtype=jnp.int32)
    flip = jax.random.randint(third_key, shape, 0, 2, dtype=jnp.int32)
    flip = flip.at[0, 0].set(0)
    upper = jnp.where(flip == 1, light, heavy)
    lower = jnp.where(flip == 1, heavy, light)
    paired = jnp.stack([upper, lower], axis=1)
    return paired.reshape(N_LEND, N_WIDE).astype(jnp.int32)


def with_ends(values, stream_key, smallest, top_value):
    longest = values.shape.index(max(values.shape))
    spots = []
    for shift in (0, 1):
        where = [jax.random.randint(jax.random.fold_in(stream_key, axis), (), 0, length) for axis, length in enumerate(values.shape)]
        where[longest] = (where[longest] + shift) % values.shape[longest]
        spots.append(tuple(where))
    return values.at[spots[0]].set(smallest).at[spots[1]].set(top_value)


def block_scale(rng, extent, shards, low, largest):
    loudness = 1.0
    for axis_at, parts in shards:
        heights = jax.random.uniform(jax.random.fold_in(jax.random.fold_in(rng, 6), axis_at), (parts,), jnp.float32, low / len(shards), largest / len(shards))
        loudness = loudness * jnp.repeat(jnp.exp(heights), extent[axis_at] // parts).reshape((-1,) + (1,) * (len(extent) - 1 - axis_at))
    return loudness


def noise(key, dims, width, bound, cuts=(), held_as=jnp.bfloat16):
    factor_of = block_scale(key, dims, cuts, -0.22, 0.18) if cuts else 1.0
    entries = jax.random.normal(key, dims, jnp.float32) * width * factor_of
    return jnp.minimum(jnp.maximum(entries, -bound), bound).astype(held_as)


def setup_inputs(seed: int = 0) -> dict:
    streams_of = jax.random.split(jax.random.key(seed), 5)
    operators = draw_operators(jax.random.fold_in(streams_of[4], 71), 0)
    dual_rhs = noise(streams_of[1], (N_LEND, MULTS, K), 1.0, 6.0, ((0, 4), (1, 8)), jnp.float32)
    contact = with_ends((jax.random.randint(streams_of[2], (N_LEND, MULTS), 0, 2) < 1).astype(jnp.int32), jax.random.fold_in(streams_of[2], 1), 0, 1)
    costs = draw_costs(jax.random.fold_in(streams_of[4], 71), 0)
    return {"operators": operators, "dual_rhs": dual_rhs, "contact": contact, "costs": costs}


RIDGE = 1.0
FIRST_STEP = 0.1
EPSILON = 1e-6


def project(values, contact):
    return jnp.where(contact[..., None] == 1, jnp.maximum(values, 0.0), values)


def dual_apply(operators, costs, field):
    blocks = field.reshape(N_LEND, N_WIDE, FACE, K).astype(jnp.bfloat16)
    previous = jnp.roll(blocks, 1, axis=1)
    operand = jnp.concatenate([-previous, blocks], axis=2)
    slots = jnp.arange(M, dtype=jnp.int32)
    active = slots[None, None, :, None] < (costs * ROWBLK)[:, :, None, None]
    operand = jnp.where(active, operand, jnp.zeros_like(operand))

    def single(items):
        matrix, vectors, keep = items
        product = jnp.dot(matrix, vectors, preferred_element_type=jnp.float32)
        return jnp.where(keep, product, jnp.float32(0.0))

    products = lax.map(single, (operators.reshape(N_LEND * N_WIDE, M, M), operand.reshape(N_LEND * N_WIDE, M, K), active.reshape(N_LEND * N_WIDE, M, 1)))
    products = products.reshape(N_LEND, N_WIDE, M, K)
    summed = products[:, :, FACE:, :] - jnp.roll(products[:, :, :FACE, :], -1, axis=1)
    return summed.reshape(N_LEND, MULTS, K) + RIDGE * field


def reference(operators, dual_rhs, contact, costs):
    multipliers = jnp.zeros(dual_rhs.shape, jnp.float32)
    image = jnp.zeros(dual_rhs.shape, jnp.float32)
    gradient = -dual_rhs
    steplen = jnp.full((N_LEND, 1, K), FIRST_STEP, jnp.float32)
    for iteration in range(ITERS):
        moved = project(multipliers - steplen * gradient, contact)
        change = moved - multipliers
        response = dual_apply(operators, costs, change)
        image = image + response
        gradient = image - dual_rhs
        multipliers = moved
        if iteration + 1 < ITERS:
            numer = jnp.sum(change * change, axis=1, keepdims=True)
            denom = jnp.sum(change * response, axis=1, keepdims=True)
            steplen = (numer + EPSILON) / (denom + EPSILON)
    return (multipliers, gradient)
```

```python
import functools

import jax
import jax.numpy as jnp
from jax import lax
from jax.experimental import pallas as pl
from jax.experimental.pallas import tpu as pltpu
from jax.sharding import PartitionSpec as P

ROWBLK = 128
ITERS = 4
RIDGE = 1.0
FIRST_STEP = 0.1
EPSILON = 1e-06
PIECES = 2
MESH = pl.DeviceIdType.MESH


def kernel(
    n,
    op_hbm,
    rhs_hbm,
    contact_ref,
    costs_ref,
    lam_hbm,
    grad_hbm,
    op,
    rhs,
    rhs_send,
    rhs_recv,
    contact_recv,
    floor,
    lam,
    grad,
    operand,
    y_send,
    y_recv,
    part_send,
    part_recv,
    load_sem,
    out_sem,
    first_send_sem,
    first_recv_sem,
    y_send_sem,
    y_recv_sem,
    part_send_sem,
    part_recv_sem,
):
    order, cases = operand.shape
    face = order // 2
    piece = face // PIECES
    me = lax.axis_index("wide")
    right = lax.rem(me + 1, n)
    left = lax.rem(me + n - 1, n)

    load_rhs = pltpu.make_async_copy(rhs_hbm.at[0], rhs, load_sem.at[0])
    load_rhs.start()
    load_op = pltpu.make_async_copy(op_hbm.at[0, 0], op, load_sem.at[1])
    load_op.start()

    barrier = pltpu.get_barrier_semaphore()
    for d in range(1, n):
        pl.semaphore_signal(
            barrier, inc=1, device_id={"wide": lax.rem(me + d, n)}, device_id_type=MESH
        )

    live = costs_ref[0, 0] * ROWBLK

    def active(start, rows):
        return lax.broadcasted_iota(jnp.int32, (rows, cases), 0) + start < live

    def make_floor(flags, base):
        for start in range(0, face, ROWBLK):
            row = flags[:, start : start + ROWBLK]
            row = jnp.where(row == 1, 0.0, -jnp.inf).astype(jnp.float32)
            floor[base + start : base + start + ROWBLK, :] = jnp.broadcast_to(
                row, (cases, ROWBLK)
            ).T

    load_rhs.wait()
    for p in range(PIECES):
        rows = slice(p * piece, (p + 1) * piece)
        rhs_send[rows, :] = rhs[rows, :].astype(jnp.bfloat16)

    pl.semaphore_wait(barrier, n - 1)

    sent = []
    first = []
    copy = pltpu.make_async_remote_copy(
        src_ref=contact_ref,
        dst_ref=contact_recv,
        send_sem=first_send_sem.at[PIECES],
        recv_sem=first_recv_sem.at[PIECES],
        device_id={"wide": right},
        device_id_type=MESH,
    )
    copy.start()
    contact_copy = copy
    sent.append(copy)
    for p in range(PIECES):
        rows = pl.ds(p * piece, piece)
        copy = pltpu.make_async_remote_copy(
            src_ref=rhs_send.at[rows],
            dst_ref=rhs_recv.at[rows],
            send_sem=first_send_sem.at[p],
            recv_sem=first_recv_sem.at[p],
            device_id={"wide": right},
            device_id_type=MESH,
        )
        copy.start()
        first.append(copy)
        sent.append(copy)

    make_floor(contact_ref, face)
    steplen = jnp.full((1, cases), FIRST_STEP, jnp.float32)
    arrivals = None
    for it in range(ITERS):
        finished = it + 1 == ITERS
        squares = jnp.zeros((8, cases), jnp.float32)
        for own in (True, False):
            base = face if own else 0
            if it == 0 and not own:
                contact_copy.wait_recv()
                make_floor(contact_recv, 0)
            for start in range(0, face, ROWBLK):
                at = slice(base + start, base + start + ROWBLK)
                here = slice(start, start + ROWBLK)
                fresh = start % piece == 0
                if it == 0:
                    if own:
                        g = -rhs[here, :]
                    else:
                        if fresh:
                            first[start // piece].wait_recv()
                        g = -rhs_recv[here, :].astype(jnp.float32)
                    before = jnp.zeros_like(g)
                else:
                    other = 0 if own else face
                    if fresh:
                        arrivals[(other + start) // piece].wait_recv()
                    there = slice(other + start, other + start + ROWBLK)
                    came = y_recv[it - 1, there, :].astype(jnp.float32)
                    g = grad[at, :] - came if own else grad[at, :] + came
                    before = lam[at, :]
                moved = jnp.maximum(before - steplen * g, floor[at, :])
                change = moved - before
                lam[at, :] = moved
                grad[at, :] = g + RIDGE * change
                if own:
                    squares += jnp.sum(
                        (change * change).reshape(ROWBLK // 8, 8, cases), axis=0
                    )
                signed = change if own else -change
                operand[at, :] = jnp.where(
                    active(base + start, ROWBLK), signed, 0.0
                ).astype(jnp.bfloat16)
        if finished:
            save_lam = pltpu.make_async_copy(
                lam.at[pl.ds(face, face)], lam_hbm.at[0], out_sem.at[0]
            )
            save_lam.start()
        if it == 0:
            load_op.wait()
        bending = RIDGE * squares
        next_arrivals = {}
        for p in range(PIECES):
            for base in (0, face):
                start = base + p * piece
                at = slice(start, start + piece)
                vectors = operand[...]
                y = jnp.dot(op[at, :], vectors, preferred_element_type=jnp.float32)
                y = jnp.where(active(start, piece), y, 0.0)
                if not finished or base == 0:
                    y_send[it, at, :] = y.astype(jnp.bfloat16)
                    copy = pltpu.make_async_remote_copy(
                        src_ref=y_send.at[it, pl.ds(start, piece)],
                        dst_ref=y_recv.at[it, pl.ds(start, piece)],
                        send_sem=y_send_sem.at[it, start // piece],
                        recv_sem=y_recv_sem.at[it, start // piece],
                        device_id={"wide": left if base == 0 else right},
                        device_id_type=MESH,
                    )
                    copy.start()
                    sent.append(copy)
                    next_arrivals[start // piece] = copy
                if base == 0:
                    if not finished:
                        grad[at, :] = grad[at, :] - y
                else:
                    grad[at, :] = grad[at, :] + y
                if not finished:
                    bending += jnp.sum(
                        (operand[at, :].astype(jnp.float32) * y).reshape(
                            piece // 8, 8, cases
                        ),
                        axis=0,
                    )
        arrivals = next_arrivals
        if not finished:
            mine = jnp.concatenate(
                [
                    jnp.sum(squares, axis=0, keepdims=True),
                    jnp.sum(bending, axis=0, keepdims=True),
                ],
                axis=0,
            )
            part_send[it] = mine
            parts = []
            for d in range(1, n):
                copy = pltpu.make_async_remote_copy(
                    src_ref=part_send.at[it],
                    dst_ref=part_recv.at[it, d],
                    send_sem=part_send_sem.at[it, d],
                    recv_sem=part_recv_sem.at[it, d],
                    device_id={"wide": lax.rem(me + d, n)},
                    device_id_type=MESH,
                )
                copy.start()
                parts.append(copy)
                sent.append(copy)
            total = mine
            for d in range(1, n):
                parts[d - 1].wait_recv()
                total = total + part_recv[it, d]
            steplen = (total[0:1] + EPSILON) / (total[1:2] + EPSILON)

    saves = [save_lam]
    for p in range(PIECES):
        arrivals[p].wait_recv()
        at = slice(face + p * piece, face + (p + 1) * piece)
        here = slice(p * piece, (p + 1) * piece)
        grad[at, :] = grad[at, :] - y_recv[ITERS - 1, here, :].astype(jnp.float32)
        save = pltpu.make_async_copy(
            grad.at[pl.ds(face + p * piece, piece)],
            grad_hbm.at[0, pl.ds(p * piece, piece)],
            out_sem.at[1 + p],
        )
        save.start()
        saves.append(save)
    for copy in sent:
        copy.wait_send()
    for save in saves:
        save.wait()


def on_device(operators, dual_rhs, contact, costs):
    n = lax.axis_size("wide")
    order = operators.shape[2]
    face, cases = dual_rhs.shape[1:]
    f32, bf16 = jnp.float32, jnp.bfloat16
    chunks = 2 * PIECES
    shape = jax.ShapeDtypeStruct(dual_rhs.shape, f32)
    return pl.pallas_call(
        functools.partial(kernel, n),
        out_shape=(shape, shape),
        in_specs=[
            pl.BlockSpec(memory_space=pl.ANY),
            pl.BlockSpec(memory_space=pl.ANY),
            pl.BlockSpec(memory_space=pltpu.VMEM),
            pl.BlockSpec(memory_space=pltpu.SMEM),
        ],
        out_specs=(
            pl.BlockSpec(memory_space=pl.ANY),
            pl.BlockSpec(memory_space=pl.ANY),
        ),
        scratch_shapes=[
            pltpu.VMEM((order, order), bf16),
            pltpu.VMEM((face, cases), f32),
            pltpu.VMEM((face, cases), bf16),
            pltpu.VMEM((face, cases), bf16),
            pltpu.VMEM((1, face), jnp.int32),
            pltpu.VMEM((order, cases), f32),
            pltpu.VMEM((order, cases), f32),
            pltpu.VMEM((order, cases), f32),
            pltpu.VMEM((order, cases), bf16),
            pltpu.VMEM((ITERS, order, cases), bf16),
            pltpu.VMEM((ITERS, order, cases), bf16),
            pltpu.VMEM((ITERS, 2, cases), f32),
            pltpu.VMEM((ITERS, n, 2, cases), f32),
            pltpu.SemaphoreType.DMA((2,)),
            pltpu.SemaphoreType.DMA((1 + PIECES,)),
            pltpu.SemaphoreType.DMA((1 + PIECES,)),
            pltpu.SemaphoreType.DMA((1 + PIECES,)),
            pltpu.SemaphoreType.DMA((ITERS, chunks)),
            pltpu.SemaphoreType.DMA((ITERS, chunks)),
            pltpu.SemaphoreType.DMA((ITERS, n)),
            pltpu.SemaphoreType.DMA((ITERS, n)),
        ],
        compiler_params=pltpu.CompilerParams(
            collective_id=0,
            has_side_effects=True,
            vmem_limit_bytes=60 * 1024 * 1024,
        ),
        cost_estimate=pl.CostEstimate(
            flops=2 * ITERS * order * order * cases,
            bytes_accessed=2 * order * order + 12 * face * cases,
            transcendentals=0,
        ),
    )(operators, dual_rhs, contact, costs)


def solution(mesh):
    return jax.shard_map(
        on_device,
        mesh=mesh,
        in_specs=(
            P("lend", "wide", None, None),
            P("lend", "wide", None),
            P("lend", "wide"),
            P("lend", "wide"),
        ),
        out_specs=(P("lend", "wide", None), P("lend", "wide", None)),
        check_vma=False,
    )
```

```python
import functools

import jax
import jax.numpy as jnp
from jax import lax
from jax.experimental import pallas as pl
from jax.experimental.pallas import tpu as pltpu
from jax.sharding import PartitionSpec as P

ROWBLK = 128
ITERS = 4
RIDGE = 1.0
FIRST_STEP = 0.1
EPSILON = 1e-06
PIECES = 2
MESH = pl.DeviceIdType.MESH


def kernel(
    n,
    op_hbm,
    rhs_hbm,
    contact_ref,
    costs_ref,
    lam_hbm,
    grad_hbm,
    op,
    rhs,
    rhs_send,
    rhs_recv,
    facts_send,
    facts_recv,
    floor,
    lam,
    grad,
    operand,
    product,
    y_send,
    top_recv,
    pair_recv,
    low_send,
    low_recv,
    part_send,
    part_recv,
    load_sem,
    out_sem,
    first_send_sem,
    first_recv_sem,
    top_send_sem,
    top_recv_sem,
    low_send_sem,
    low_recv_sem,
    part_send_sem,
    part_recv_sem,
):
    order, cases = operand.shape
    face = order // 2
    piece = face // PIECES
    me = lax.axis_index("wide")
    right = {"wide": lax.rem(me + 1, n)}
    left = {"wide": lax.rem(me + n - 1, n)}
    lend = lax.axis_index("lend")
    side = lax.rem(lend, 2)
    pair = {"lend": lend + 1 - 2 * side}
    mine = pl.ds(pl.multiple_of(side * piece, piece), piece)
    theirs = pl.ds(pl.multiple_of((1 - side) * piece, piece), piece)
    sent = []

    def send(src, dst, send_sem, recv_sem, where):
        copy = pltpu.make_async_remote_copy(
            src_ref=src,
            dst_ref=dst,
            send_sem=send_sem,
            recv_sem=recv_sem,
            device_id=where,
            device_id_type=MESH,
        )
        copy.start()
        sent.append(copy)
        return copy

    load_rhs = pltpu.make_async_copy(rhs_hbm.at[0], rhs, load_sem.at[0])
    load_rhs.start()
    load_op = pltpu.make_async_copy(op_hbm.at[0, 0], op, load_sem.at[1])
    load_op.start()

    barrier = pltpu.get_barrier_semaphore()
    for d in range(1, n):
        pl.semaphore_signal(
            barrier, inc=1, device_id={"wide": lax.rem(me + d, n)}, device_id_type=MESH
        )
    pl.semaphore_signal(barrier, inc=1, device_id=pair, device_id_type=MESH)

    live = costs_ref[0, 0] * ROWBLK

    def active(start, rows, count):
        return lax.broadcasted_iota(jnp.int32, (rows, cases), 0) + start < count

    def make_floor(flags, base):
        for start in range(0, face, ROWBLK):
            row = flags[0:1, start : start + ROWBLK]
            row = jnp.where(row == 1, 0.0, -jnp.inf).astype(jnp.float32)
            floor[base + start : base + start + ROWBLK, :] = jnp.broadcast_to(
                row, (cases, ROWBLK)
            ).T

    facts_send[0:1, :] = contact_ref[...]
    facts_send[1:2, :] = jnp.full((1, face), live, jnp.int32)
    load_rhs.wait()
    rhs_send[...] = rhs[...].astype(jnp.bfloat16)

    pl.semaphore_wait(barrier, n)

    facts = send(
        facts_send, facts_recv, first_send_sem.at[PIECES], first_recv_sem.at[PIECES], right
    )
    first = []
    for p in range(PIECES):
        rows = pl.ds(p * piece, piece)
        first.append(
            send(
                rhs_send.at[rows],
                rhs_recv.at[rows],
                first_send_sem.at[p],
                first_recv_sem.at[p],
                right,
            )
        )

    def advance(base, start, rows, steplen, gradient_at, begins):
        squares = jnp.zeros((8, cases), jnp.float32)
        for here in range(start, start + rows, ROWBLK):
            at = slice(base + here, base + here + ROWBLK)
            g = gradient_at(here)
            before = jnp.zeros_like(g) if begins else lam[at, :]
            moved = jnp.maximum(before - steplen * g, floor[at, :])
            change = moved - before
            lam[at, :] = moved
            grad[at, :] = g + RIDGE * change
            squares += jnp.sum((change * change).reshape(ROWBLK // 8, 8, cases), axis=0)
            signed = change if base else -change
            operand[at, :] = jnp.where(
                active(base + here, ROWBLK, live), signed, 0.0
            ).astype(jnp.bfloat16)
        return squares

    def multiply(start, columns, begins):
        vectors = operand[start : start + columns, :]
        for r in range(0, order, piece):
            part = jnp.dot(
                op[r : r + piece, start : start + columns],
                vectors,
                preferred_element_type=jnp.float32,
            )
            at = slice(r, r + piece)
            product[at, :] = part if begins else product[at, :] + part

    make_floor(contact_ref, face)
    steplen = jnp.full((1, cases), FIRST_STEP, jnp.float32)
    tops = lows = None
    live_left = None
    for it in range(ITERS):
        finished = it + 1 == ITERS
        if it == 0:
            squares = advance(face, 0, face, steplen, lambda i: -rhs[i : i + ROWBLK, :], True)
            load_op.wait()
            multiply(face, face, True)
            facts.wait_recv()
            make_floor(facts_recv, 0)
            live_left = facts_recv[1:2, 0:cases]
            for p in range(PIECES):
                first[p].wait_recv()
                advance(
                    0,
                    p * piece,
                    piece,
                    steplen,
                    lambda i: -rhs_recv[i : i + ROWBLK, :].astype(jnp.float32),
                    True,
                )
                if p + 1 < PIECES:
                    multiply(p * piece, piece, False)
            last = (PIECES - 1) * piece
        else:

            def own_gradient(i, it=it):
                came = top_recv[it - 1, i : i + ROWBLK, :].astype(jnp.float32)
                return grad[face + i : face + i + ROWBLK, :] - came

            def left_gradient(i, it=it):
                came = low_recv[it - 1, i : i + ROWBLK, :].astype(jnp.float32)
                came = jnp.where(active(face + i, ROWBLK, live_left), came, 0.0)
                return grad[i : i + ROWBLK, :] + came

            squares = jnp.zeros((8, cases), jnp.float32)
            for p in range(PIECES):
                if p + 1 == PIECES:
                    lows.wait_recv()
                    forward = send(
                        low_recv.at[it - 1, mine],
                        low_recv.at[it - 1, mine],
                        low_send_sem.at[it - 1, 2],
                        low_recv_sem.at[it - 1, 2],
                        pair,
                    )
                    forward.wait_recv()
                    advance(0, 0, face, steplen, left_gradient, False)
                    multiply(0, face, False)
                tops[p].wait_recv()
                squares += advance(face, p * piece, piece, steplen, own_gradient, False)
                if p + 1 < PIECES:
                    multiply(face + p * piece, piece, p == 0)
            last = face + (PIECES - 1) * piece
        if finished:
            save_lam = pltpu.make_async_copy(
                lam.at[pl.ds(face, face)], lam_hbm.at[0], out_sem.at[0]
            )
            save_lam.start()

        bending = RIDGE * squares
        tops = []
        vectors = operand[last : last + piece, :]
        for r in list(range(face, order, piece)) + list(range(0, face, piece)):
            at = slice(r, r + piece)
            y = product[at, :] + jnp.dot(
                op[at, last : last + piece], vectors, preferred_element_type=jnp.float32
            )
            y = jnp.where(active(r, piece, live), y, 0.0)
            product[at, :] = y
            if finished and r >= face:
                continue
            y_send[it, at, :] = y.astype(jnp.bfloat16)
            if not finished:
                bending += jnp.sum(
                    (operand[at, :].astype(jnp.float32) * y).reshape(
                        piece // 8, 8, cases
                    ),
                    axis=0,
                )
                if r + piece == order:
                    swap = send(
                        y_send.at[it, pl.ds(pl.multiple_of(face + (1 - side) * piece, piece), piece)],
                        pair_recv.at[it],
                        low_send_sem.at[it, 0],
                        low_recv_sem.at[it, 0],
                        pair,
                    )

        def send_top(p):
            rows = pl.ds(p * piece, piece)
            tops.append(
                send(
                    y_send.at[it, rows],
                    top_recv.at[it, rows],
                    top_send_sem.at[it, p],
                    top_recv_sem.at[it, p],
                    left,
                )
            )

        if finished:
            for p in range(PIECES):
                send_top(p)
            grad[face:, :] = grad[face:, :] + product[face:, :]
        else:
            own = jnp.concatenate(
                [
                    jnp.sum(squares, axis=0, keepdims=True),
                    jnp.sum(bending, axis=0, keepdims=True),
                ],
                axis=0,
            )
            part_send[it] = own
            parts = [
                send(
                    part_send.at[it],
                    part_recv.at[it, d],
                    part_send_sem.at[it, d],
                    part_recv_sem.at[it, d],
                    {"wide": lax.rem(me + d, n)},
                )
                for d in range(1, n)
            ]
            for p in range(PIECES - 1):
                send_top(p)
            swap.wait_recv()
            low_mine = pl.ds(pl.multiple_of(face + side * piece, piece), piece)
            low_send[it] = y_send[it, low_mine, :] + pair_recv[it]
            lows = send(
                low_send.at[it],
                low_recv.at[it, mine],
                low_send_sem.at[it, 1],
                low_recv_sem.at[it, 1],
                right,
            )
            send_top(PIECES - 1)
            grad[:face, :] = grad[:face, :] - product[:face, :]
            grad[face:, :] = grad[face:, :] + product[face:, :]
            total = own
            for d in range(1, n):
                parts[d - 1].wait_recv()
                total = total + part_recv[it, d]
            steplen = (total[0:1] + EPSILON) / (total[1:2] + EPSILON)

    saves = [save_lam]
    for p in range(PIECES):
        tops[p].wait_recv()
        at = slice(face + p * piece, face + (p + 1) * piece)
        here = slice(p * piece, (p + 1) * piece)
        grad[at, :] = grad[at, :] - top_recv[ITERS - 1, here, :].astype(jnp.float32)
        save = pltpu.make_async_copy(
            grad.at[pl.ds(face + p * piece, piece)],
            grad_hbm.at[0, pl.ds(p * piece, piece)],
            out_sem.at[1 + p],
        )
        save.start()
        saves.append(save)
    for copy in sent:
        copy.wait_send()
    for save in saves:
        save.wait()


def on_device(operators, dual_rhs, contact, costs):
    n = lax.axis_size("wide")
    order = operators.shape[2]
    face, cases = dual_rhs.shape[1:]
    f32, bf16 = jnp.float32, jnp.bfloat16
    piece = face // PIECES
    shape = jax.ShapeDtypeStruct(dual_rhs.shape, f32)
    return pl.pallas_call(
        functools.partial(kernel, n),
        out_shape=(shape, shape),
        in_specs=[
            pl.BlockSpec(memory_space=pl.ANY),
            pl.BlockSpec(memory_space=pl.ANY),
            pl.BlockSpec(memory_space=pltpu.VMEM),
            pl.BlockSpec(memory_space=pltpu.SMEM),
        ],
        out_specs=(
            pl.BlockSpec(memory_space=pl.ANY),
            pl.BlockSpec(memory_space=pl.ANY),
        ),
        scratch_shapes=[
            pltpu.VMEM((order, order), bf16),
            pltpu.VMEM((face, cases), f32),
            pltpu.VMEM((face, cases), bf16),
            pltpu.VMEM((face, cases), bf16),
            pltpu.VMEM((2, face), jnp.int32),
            pltpu.VMEM((2, face), jnp.int32),
            pltpu.VMEM((order, cases), f32),
            pltpu.VMEM((order, cases), f32),
            pltpu.VMEM((order, cases), f32),
            pltpu.VMEM((order, cases), bf16),
            pltpu.VMEM((order, cases), f32),
            pltpu.VMEM((ITERS, order, cases), bf16),
            pltpu.VMEM((ITERS, face, cases), bf16),
            pltpu.VMEM((ITERS, piece, cases), bf16),
            pltpu.VMEM((ITERS, piece, cases), bf16),
            pltpu.VMEM((ITERS, face, cases), bf16),
            pltpu.VMEM((ITERS, 2, cases), f32),
            pltpu.VMEM((ITERS, n, 2, cases), f32),
            pltpu.SemaphoreType.DMA((2,)),
            pltpu.SemaphoreType.DMA((1 + PIECES,)),
            pltpu.SemaphoreType.DMA((1 + PIECES,)),
            pltpu.SemaphoreType.DMA((1 + PIECES,)),
            pltpu.SemaphoreType.DMA((ITERS, PIECES)),
            pltpu.SemaphoreType.DMA((ITERS, PIECES)),
            pltpu.SemaphoreType.DMA((ITERS, 3)),
            pltpu.SemaphoreType.DMA((ITERS, 3)),
            pltpu.SemaphoreType.DMA((ITERS, n)),
            pltpu.SemaphoreType.DMA((ITERS, n)),
        ],
        compiler_params=pltpu.CompilerParams(
            collective_id=0,
            has_side_effects=True,
            vmem_limit_bytes=52 * 1024 * 1024,
        ),
        cost_estimate=pl.CostEstimate(
            flops=2 * ITERS * order * order * cases,
            bytes_accessed=2 * order * order + 12 * face * cases,
            transcendentals=0,
        ),
    )(operators, dual_rhs, contact, costs)


def solution(mesh):
    return jax.shard_map(
        on_device,
        mesh=mesh,
        in_specs=(
            P("lend", "wide", None, None),
            P("lend", "wide", None),
            P("lend", "wide"),
            P("lend", "wide"),
        ),
        out_specs=(P("lend", "wide", None), P("lend", "wide", None)),
        check_vma=False,
    )
```

```python
import functools

import jax
import jax.numpy as jnp
from jax import lax
from jax.experimental import pallas as pl
from jax.experimental.pallas import tpu as pltpu
from jax.sharding import PartitionSpec as P

ROWBLK = 128
ITERS = 4
RIDGE = 1.0
FIRST_STEP = 0.1
EPSILON = 1e-06
PARTS = 2
MESH = pl.DeviceIdType.MESH


def kernel(
    n,
    op_hbm,
    rhs_hbm,
    contact_hbm,
    costs_ref,
    lam_hbm,
    grad_hbm,
    op,
    rhs,
    own_rhs,
    rhs_send,
    rhs_recv,
    contact,
    contact_recv,
    floor,
    lam,
    grad,
    field,
    operand,
    out,
    y_send,
    top_recv,
    low_recv,
    part_send,
    part_recv,
    load_sem,
    out_sem,
    first_send_sem,
    first_recv_sem,
    y_send_sem,
    y_recv_sem,
    part_send_sem,
    part_recv_sem,
):
    order = op.shape[0]
    face, cases = rhs.shape
    rows = face // PARTS
    me = lax.axis_index("wide")
    right = {"wide": lax.rem(me + 1, n)}
    left = {"wide": lax.rem(me + n - 1, n)}
    sent = []

    def send(src, dst, send_sem, recv_sem, where):
        copy = pltpu.make_async_remote_copy(
            src_ref=src,
            dst_ref=dst,
            send_sem=send_sem,
            recv_sem=recv_sem,
            device_id=where,
            device_id_type=MESH,
        )
        copy.start()
        sent.append(copy)
        return copy

    load_rhs = pltpu.make_async_copy(rhs_hbm.at[0], rhs, load_sem.at[0])
    load_rhs.start()
    load_contact = pltpu.make_async_copy(contact_hbm, contact, load_sem.at[1])
    load_contact.start()
    load_op = pltpu.make_async_copy(op_hbm.at[0, 0], op, load_sem.at[2])
    load_op.start()

    barrier = pltpu.get_barrier_semaphore()
    for d in range(1, n):
        pl.semaphore_signal(
            barrier, inc=1, device_id={"wide": lax.rem(me + d, n)}, device_id_type=MESH
        )

    def first_lanes(count):
        return lax.broadcasted_iota(jnp.int32, (count, cases), 1) < cases // 2

    def swap(values):
        return pltpu.roll(values, cases // 2, axis=1)

    def active(start, count):
        row = lax.broadcasted_iota(jnp.int32, (count, cases), 0) + start
        return jnp.where(first_lanes(count), row, row + rows) < live

    def exchange(upper, lower, half):
        first = first_lanes(upper.shape[0])
        if half == 0:
            return jnp.where(first, upper, swap(lower))
        return jnp.where(first, swap(upper), lower)

    def make_floor(flags, base):
        for start in range(0, rows, ROWBLK):
            both = [
                jnp.broadcast_to(
                    jnp.where(flags[0:1, at : at + ROWBLK] == 1, 0.0, -jnp.inf).astype(
                        jnp.float32
                    ),
                    (cases // 2, ROWBLK),
                )
                for at in (start, start + rows)
            ]
            floor[base + start : base + start + ROWBLK, :] = jnp.concatenate(
                both, axis=0
            ).T

    load_rhs.wait()
    for half in range(2):
        packed = exchange(rhs[0:rows, :], rhs[rows:face, :], half)
        own_rhs[half] = packed
        rhs_send[half] = packed.astype(jnp.bfloat16)
    load_contact.wait()
    live = costs_ref[0, 0] * ROWBLK

    pl.semaphore_wait(barrier, n - 1)

    first = [
        send(
            rhs_send.at[half],
            rhs_recv.at[half],
            first_send_sem.at[half],
            first_recv_sem.at[half],
            right,
        )
        for half in range(2)
    ]
    facts = send(contact, contact_recv, first_send_sem.at[2], first_recv_sem.at[2], right)

    def advance(half, own, steplen, gradient_at, begins):
        base = rows if own else 0
        squares = jnp.zeros((8, cases), jnp.float32)
        for here in range(0, rows, ROWBLK):
            at = slice(base + here, base + here + ROWBLK)
            g = gradient_at(here)
            before = jnp.zeros_like(g) if begins else lam[half, at, :]
            moved = jnp.maximum(before - steplen * g, floor[at, :])
            change = moved - before
            lam[half, at, :] = moved
            grad[half, at, :] = g + RIDGE * change
            if own:
                squares += jnp.sum(
                    (change * change).reshape(ROWBLK // 8, 8, cases), axis=0
                )
            masked = jnp.where(
                active(2 * base + here, ROWBLK), change if own else -change, 0.0
            )
            field[half, at, :] = masked
            turned = swap(masked)
            lanes = first_lanes(ROWBLK)
            slot = 2 * base + here
            operand[half, slot : slot + ROWBLK, :] = jnp.where(
                lanes, masked, turned
            ).astype(jnp.bfloat16)
            operand[half, slot + rows : slot + rows + ROWBLK, :] = jnp.where(
                lanes, turned, masked
            ).astype(jnp.bfloat16)
        return squares

    def fold(sums):
        total = jnp.sum(sums, axis=0, keepdims=True)
        return total + swap(total)

    steplen = [jnp.full((1, cases), FIRST_STEP, jnp.float32)] * 2
    make_floor(contact, rows)
    squares = [
        advance(
            half,
            True,
            steplen[half],
            lambda i, half=half: -own_rhs[half, i : i + ROWBLK, :],
            True,
        )
        for half in range(2)
    ]
    facts.wait_recv()
    make_floor(contact_recv, 0)
    tops, lows, parts, sums = [None] * 2, [None] * 2, [None] * 2, [None] * 2
    for it in range(ITERS):
        finished = it + 1 == ITERS
        for half in range(2):
            if it == 0:
                first[half].wait_recv()
                advance(
                    half,
                    False,
                    steplen[half],
                    lambda i: -rhs_recv[half, i : i + ROWBLK, :].astype(jnp.float32),
                    True,
                )
            else:
                total = sums[half]
                for d in range(1, n):
                    parts[half][d - 1].wait_recv()
                    total = total + part_recv[it - 1, half, d]
                steplen[half] = (total[0:1] + EPSILON) / (total[1:2] + EPSILON)

                def own_gradient(i):
                    came = top_recv[it - 1, half, i : i + ROWBLK, :]
                    at = slice(rows + i, rows + i + ROWBLK)
                    return grad[half, at, :] - came.astype(jnp.float32)

                def left_gradient(i):
                    came = low_recv[it - 1, half, i : i + ROWBLK, :]
                    at = slice(i, i + ROWBLK)
                    return grad[half, at, :] + came.astype(jnp.float32)

                tops[half].wait_recv()
                squares[half] = advance(half, True, steplen[half], own_gradient, False)
                lows[half].wait_recv()
                advance(half, False, steplen[half], left_gradient, False)
            if it == 0 and half == 0:
                load_op.wait()

            bending = RIDGE * squares[half]
            for base in (0, rows):
                y = jnp.dot(
                    op[2 * base : 2 * base + face, :],
                    operand[half],
                    preferred_element_type=jnp.float32,
                )
                y = jnp.where(first_lanes(rows), y[0:rows, :], y[rows:face, :])
                y = jnp.where(active(2 * base, rows), y, 0.0)
                at = slice(base, base + rows)
                if not finished or base == 0:
                    y_send[it, half, at, :] = y.astype(jnp.bfloat16)
                if base == 0:
                    tops[half] = send(
                        y_send.at[it, half, pl.ds(0, rows)],
                        top_recv.at[it, half],
                        y_send_sem.at[it, half, 0],
                        y_recv_sem.at[it, half, 0],
                        left,
                    )
                    if not finished:
                        grad[half, at, :] = grad[half, at, :] - y
                else:
                    grad[half, at, :] = grad[half, at, :] + y
                if not finished:
                    bending += jnp.sum(
                        (field[half, at, :] * y).reshape(rows // 8, 8, cases), axis=0
                    )
            if finished:
                continue
            sums[half] = jnp.concatenate([fold(squares[half]), fold(bending)], axis=0)
            part_send[it, half] = sums[half]
            parts[half] = [
                send(
                    part_send.at[it, half],
                    part_recv.at[it, half, d],
                    part_send_sem.at[it, half, d],
                    part_recv_sem.at[it, half, d],
                    {"wide": lax.rem(me + d, n)},
                )
                for d in range(1, n)
            ]
            lows[half] = send(
                y_send.at[it, half, pl.ds(rows, rows)],
                low_recv.at[it, half],
                y_send_sem.at[it, half, 1],
                y_recv_sem.at[it, half, 1],
                right,
            )

    def unpack(source):
        return [
            exchange(source[0, rows:face, :], source[1, rows:face, :], part)
            for part in range(2)
        ]

    saves = []

    def save(number, values, target):
        for part in range(2):
            out[number, part * rows : (part + 1) * rows, :] = values[part]
        copy = pltpu.make_async_copy(out.at[number], target.at[0], out_sem.at[number])
        copy.start()
        saves.append(copy)

    save(0, unpack(lam), lam_hbm)
    for half in range(2):
        tops[half].wait_recv()
        came = top_recv[ITERS - 1, half].astype(jnp.float32)
        grad[half, rows:face, :] = grad[half, rows:face, :] - came
    save(1, unpack(grad), grad_hbm)
    for copy in sent:
        copy.wait_send()
    for copy in saves:
        copy.wait()


def write_out(lam, grad, lam_out, grad_out, sem):
    copies = [
        pltpu.make_async_copy(lam, lam_out, sem.at[0]),
        pltpu.make_async_copy(grad, grad_out, sem.at[1]),
    ]
    for copy in copies:
        copy.start()
    for copy in copies:
        copy.wait()


def on_device(operators, dual_rhs, contact, costs):
    n = lax.axis_size("wide")
    order = operators.shape[2]
    face, cases = dual_rhs.shape[1:]
    rows = face // PARTS
    f32, bf16 = jnp.float32, jnp.bfloat16
    shape = jax.ShapeDtypeStruct(dual_rhs.shape, f32)
    inputs = [
        pltpu.with_memory_space_constraint(x, pltpu.HBM)
        for x in (operators, dual_rhs, contact)
    ]
    results = pl.pallas_call(
        functools.partial(kernel, n),
        out_shape=(shape, shape),
        in_specs=[
            pl.BlockSpec(memory_space=pl.ANY),
            pl.BlockSpec(memory_space=pl.ANY),
            pl.BlockSpec(memory_space=pl.ANY),
            pl.BlockSpec(memory_space=pltpu.SMEM),
        ],
        out_specs=(
            pl.BlockSpec(memory_space=pl.ANY),
            pl.BlockSpec(memory_space=pl.ANY),
        ),
        scratch_shapes=[
            pltpu.VMEM((order, order), bf16),
            pltpu.VMEM((face, cases), f32),
            pltpu.VMEM((2, rows, cases), f32),
            pltpu.VMEM((2, rows, cases), bf16),
            pltpu.VMEM((2, rows, cases), bf16),
            pltpu.VMEM((1, face), jnp.int32),
            pltpu.VMEM((1, face), jnp.int32),
            pltpu.VMEM((face, cases), f32),
            pltpu.VMEM((2, face, cases), f32),
            pltpu.VMEM((2, face, cases), f32),
            pltpu.VMEM((2, face, cases), f32),
            pltpu.VMEM((2, order, cases), bf16),
            pltpu.VMEM((2, face, cases), f32),
            pltpu.VMEM((ITERS, 2, face, cases), bf16),
            pltpu.VMEM((ITERS, 2, rows, cases), bf16),
            pltpu.VMEM((ITERS, 2, rows, cases), bf16),
            pltpu.VMEM((ITERS, 2, 2, cases), f32),
            pltpu.VMEM((ITERS, 2, n, 2, cases), f32),
            pltpu.SemaphoreType.DMA((3,)),
            pltpu.SemaphoreType.DMA((2,)),
            pltpu.SemaphoreType.DMA((3,)),
            pltpu.SemaphoreType.DMA((3,)),
            pltpu.SemaphoreType.DMA((ITERS, 2, 2)),
            pltpu.SemaphoreType.DMA((ITERS, 2, 2)),
            pltpu.SemaphoreType.DMA((ITERS, 2, n)),
            pltpu.SemaphoreType.DMA((ITERS, 2, n)),
        ],
        compiler_params=pltpu.CompilerParams(
            collective_id=0,
            has_side_effects=True,
            vmem_limit_bytes=52 * 1024 * 1024,
        ),
        cost_estimate=pl.CostEstimate(
            flops=2 * ITERS * order * order * cases,
            bytes_accessed=2 * order * order + 12 * face * cases,
            transcendentals=0,
        ),
    )(*inputs, costs)
    return pl.pallas_call(
        write_out,
        out_shape=(shape, shape),
        in_specs=[pl.BlockSpec(memory_space=pl.ANY)] * 2,
        out_specs=(pl.BlockSpec(memory_space=pl.ANY),) * 2,
        scratch_shapes=[pltpu.SemaphoreType.DMA((2,))],
    )(*results)


def solution(mesh):
    return jax.shard_map(
        on_device,
        mesh=mesh,
        in_specs=(
            P("lend", "wide", None, None),
            P("lend", "wide", None),
            P("lend", "wide"),
            P("lend", "wide"),
        ),
        out_specs=(P("lend", "wide", None), P("lend", "wide", None)),
        check_vma=False,
    )
```

```python
import functools

import jax
import jax.numpy as jnp
from jax import lax
from jax.experimental import pallas as pl
from jax.experimental.pallas import tpu as pltpu
from jax.sharding import PartitionSpec as P

ROWBLK = 128
ITERS = 4
RIDGE = 1.0
FIRST_STEP = 0.1
EPSILON = 1e-06
PARTS = 2
MESH = pl.DeviceIdType.MESH


def kernel(
    n,
    op_hbm,
    rhs_hbm,
    contact_hbm,
    costs_ref,
    lam_hbm,
    grad_hbm,
    op,
    rhs,
    own_rhs,
    rhs_send,
    rhs_recv,
    contact,
    facts_send,
    facts_recv,
    floor,
    lam,
    grad,
    field,
    operand,
    out,
    y_send,
    top_recv,
    pair_recv,
    low_send,
    low_recv,
    part_send,
    part_recv,
    load_sem,
    out_sem,
    first_send_sem,
    first_recv_sem,
    y_send_sem,
    y_recv_sem,
    low_send_sem,
    low_recv_sem,
    part_send_sem,
    part_recv_sem,
):
    order = op.shape[0]
    face, cases = rhs.shape
    rows = face // PARTS
    me = lax.axis_index("wide")
    right = {"wide": lax.rem(me + 1, n)}
    left = {"wide": lax.rem(me + n - 1, n)}
    lend = lax.axis_index("lend")
    side = lax.rem(lend, 2)
    pair = {"lend": lend + 1 - 2 * side}
    share = rows // 2
    mine = pl.multiple_of(side * share, share)
    theirs = pl.multiple_of((1 - side) * share, share)
    sent = []

    def send(src, dst, send_sem, recv_sem, where):
        copy = pltpu.make_async_remote_copy(
            src_ref=src,
            dst_ref=dst,
            send_sem=send_sem,
            recv_sem=recv_sem,
            device_id=where,
            device_id_type=MESH,
        )
        copy.start()
        sent.append(copy)
        return copy

    load_rhs = pltpu.make_async_copy(rhs_hbm.at[0], rhs, load_sem.at[0])
    load_rhs.start()
    load_contact = pltpu.make_async_copy(contact_hbm, contact, load_sem.at[1])
    load_contact.start()
    load_op = pltpu.make_async_copy(op_hbm.at[0, 0], op, load_sem.at[2])
    load_op.start()

    barrier = pltpu.get_barrier_semaphore()
    for d in range(1, n):
        pl.semaphore_signal(
            barrier, inc=1, device_id={"wide": lax.rem(me + d, n)}, device_id_type=MESH
        )

    pl.semaphore_signal(barrier, inc=1, device_id=pair, device_id_type=MESH)

    def first_lanes(count):
        return lax.broadcasted_iota(jnp.int32, (count, cases), 1) < cases // 2

    def swap(values):
        return pltpu.roll(values, cases // 2, axis=1)

    def active(start, count, bound):
        row = lax.broadcasted_iota(jnp.int32, (count, cases), 0) + start
        return jnp.where(first_lanes(count), row, row + rows) < bound

    def exchange(upper, lower, half):
        first = first_lanes(upper.shape[0])
        if half == 0:
            return jnp.where(first, upper, swap(lower))
        return jnp.where(first, swap(upper), lower)

    def make_floor(flags, base):
        for start in range(0, rows, ROWBLK):
            both = [
                jnp.broadcast_to(
                    jnp.where(flags[0:1, at : at + ROWBLK] == 1, 0.0, -jnp.inf).astype(
                        jnp.float32
                    ),
                    (cases // 2, ROWBLK),
                )
                for at in (start, start + rows)
            ]
            floor[base + start : base + start + ROWBLK, :] = jnp.concatenate(
                both, axis=0
            ).T

    load_rhs.wait()
    for half in range(2):
        packed = exchange(rhs[0:rows, :], rhs[rows:face, :], half)
        own_rhs[half] = packed
        rhs_send[half] = packed.astype(jnp.bfloat16)
    load_contact.wait()
    live = costs_ref[0, 0] * ROWBLK
    facts_send[0:1, :] = contact[...]
    facts_send[1:2, :] = jnp.full((1, face), live, jnp.int32)

    pl.semaphore_wait(barrier, n)

    first = [
        send(
            rhs_send.at[half],
            rhs_recv.at[half],
            first_send_sem.at[half],
            first_recv_sem.at[half],
            right,
        )
        for half in range(2)
    ]
    facts = send(facts_send, facts_recv, first_send_sem.at[2], first_recv_sem.at[2], right)

    def advance(half, own, steplen, gradient_at, begins):
        base = rows if own else 0
        squares = jnp.zeros((8, cases), jnp.float32)
        for here in range(0, rows, ROWBLK):
            at = slice(base + here, base + here + ROWBLK)
            g = gradient_at(here)
            before = jnp.zeros_like(g) if begins else lam[half, at, :]
            moved = jnp.maximum(before - steplen * g, floor[at, :])
            change = moved - before
            lam[half, at, :] = moved
            grad[half, at, :] = g + RIDGE * change
            if own:
                squares += jnp.sum(
                    (change * change).reshape(ROWBLK // 8, 8, cases), axis=0
                )
            masked = jnp.where(
                active(2 * base + here, ROWBLK, live), change if own else -change, 0.0
            )
            field[half, at, :] = masked
            turned = swap(masked)
            lanes = first_lanes(ROWBLK)
            slot = 2 * base + here
            operand[half, slot : slot + ROWBLK, :] = jnp.where(
                lanes, masked, turned
            ).astype(jnp.bfloat16)
            operand[half, slot + rows : slot + rows + ROWBLK, :] = jnp.where(
                lanes, turned, masked
            ).astype(jnp.bfloat16)
        return squares

    def fold(sums):
        total = jnp.sum(sums, axis=0, keepdims=True)
        return total + swap(total)

    steplen = [jnp.full((1, cases), FIRST_STEP, jnp.float32)] * 2
    make_floor(contact, rows)
    squares = [
        advance(
            half,
            True,
            steplen[half],
            lambda i, half=half: -own_rhs[half, i : i + ROWBLK, :],
            True,
        )
        for half in range(2)
    ]
    facts.wait_recv()
    make_floor(facts_recv, 0)
    live_left = facts_recv[1:2, 0:cases]
    tops, swaps, lows = [None] * 2, [None] * 2, [None] * 2
    parts, sums = [None] * 2, [None] * 2
    for it in range(ITERS):
        finished = it + 1 == ITERS
        for half in range(2):
            if it == 0:
                first[half].wait_recv()
                advance(
                    half,
                    False,
                    steplen[half],
                    lambda i: -rhs_recv[half, i : i + ROWBLK, :].astype(jnp.float32),
                    True,
                )
            else:
                lows[half].wait_recv()
                forward = send(
                    low_recv.at[it - 1, half, pl.ds(mine, share)],
                    low_recv.at[it - 1, half, pl.ds(mine, share)],
                    low_send_sem.at[it - 1, half, 2],
                    low_recv_sem.at[it - 1, half, 2],
                    pair,
                )
                total = sums[half]
                for d in range(1, n):
                    parts[half][d - 1].wait_recv()
                    total = total + part_recv[it - 1, half, d]
                steplen[half] = (total[0:1] + EPSILON) / (total[1:2] + EPSILON)

                def own_gradient(i):
                    came = top_recv[it - 1, half, i : i + ROWBLK, :]
                    at = slice(rows + i, rows + i + ROWBLK)
                    return grad[half, at, :] - came.astype(jnp.float32)

                def left_gradient(i):
                    came = low_recv[it - 1, half, i : i + ROWBLK, :].astype(jnp.float32)
                    ours = active(face + i, ROWBLK, live_left)
                    at = slice(i, i + ROWBLK)
                    return grad[half, at, :] + jnp.where(ours, came, 0.0)

                tops[half].wait_recv()
                squares[half] = advance(half, True, steplen[half], own_gradient, False)
                forward.wait_recv()
                advance(half, False, steplen[half], left_gradient, False)
            if it == 0 and half == 0:
                load_op.wait()

            bending = RIDGE * squares[half]
            for base in (0, rows) if finished else (rows, 0):
                y = jnp.dot(
                    op[2 * base : 2 * base + face, :],
                    operand[half],
                    preferred_element_type=jnp.float32,
                )
                y = jnp.where(first_lanes(rows), y[0:rows, :], y[rows:face, :])
                y = jnp.where(active(2 * base, rows, live), y, 0.0)
                at = slice(base, base + rows)
                if not finished or base == 0:
                    y_send[it, half, at, :] = y.astype(jnp.bfloat16)
                if base == 0:
                    tops[half] = send(
                        y_send.at[it, half, pl.ds(0, rows)],
                        top_recv.at[it, half],
                        y_send_sem.at[it, half],
                        y_recv_sem.at[it, half],
                        left,
                    )
                    if not finished:
                        grad[half, at, :] = grad[half, at, :] - y
                else:
                    if not finished:
                        swaps[half] = send(
                            y_send.at[it, half, pl.ds(rows + theirs, share)],
                            pair_recv.at[it, half],
                            low_send_sem.at[it, half, 0],
                            low_recv_sem.at[it, half, 0],
                            pair,
                        )
                    grad[half, at, :] = grad[half, at, :] + y
                if not finished:
                    bending += jnp.sum(
                        (field[half, at, :] * y).reshape(rows // 8, 8, cases), axis=0
                    )
            if finished:
                continue
            sums[half] = jnp.concatenate([fold(squares[half]), fold(bending)], axis=0)
            part_send[it, half] = sums[half]
            parts[half] = [
                send(
                    part_send.at[it, half],
                    part_recv.at[it, half, d],
                    part_send_sem.at[it, half, d],
                    part_recv_sem.at[it, half, d],
                    {"wide": lax.rem(me + d, n)},
                )
                for d in range(1, n)
            ]
            swaps[half].wait_recv()
            low_send[it, half] = (
                y_send[it, half, pl.ds(rows + mine, share), :] + pair_recv[it, half]
            )
            lows[half] = send(
                low_send.at[it, half],
                low_recv.at[it, half, pl.ds(mine, share)],
                low_send_sem.at[it, half, 1],
                low_recv_sem.at[it, half, 1],
                right,
            )

    def unpack(source):
        return [
            exchange(source[0, rows:face, :], source[1, rows:face, :], part)
            for part in range(2)
        ]

    saves = []

    def save(number, values, target):
        for part in range(2):
            out[number, part * rows : (part + 1) * rows, :] = values[part]
        copy = pltpu.make_async_copy(out.at[number], target.at[0], out_sem.at[number])
        copy.start()
        saves.append(copy)

    save(0, unpack(lam), lam_hbm)
    for half in range(2):
        tops[half].wait_recv()
        came = top_recv[ITERS - 1, half].astype(jnp.float32)
        grad[half, rows:face, :] = grad[half, rows:face, :] - came
    save(1, unpack(grad), grad_hbm)
    for copy in sent:
        copy.wait_send()
    for copy in saves:
        copy.wait()


def on_device(operators, dual_rhs, contact, costs):
    n = lax.axis_size("wide")
    order = operators.shape[2]
    face, cases = dual_rhs.shape[1:]
    rows = face // PARTS
    f32, bf16 = jnp.float32, jnp.bfloat16
    shape = jax.ShapeDtypeStruct(dual_rhs.shape, f32)
    inputs = [
        pltpu.with_memory_space_constraint(x, pltpu.HBM)
        for x in (operators, dual_rhs, contact)
    ]
    return pl.pallas_call(
        functools.partial(kernel, n),
        out_shape=(shape, shape),
        in_specs=[
            pl.BlockSpec(memory_space=pl.ANY),
            pl.BlockSpec(memory_space=pl.ANY),
            pl.BlockSpec(memory_space=pl.ANY),
            pl.BlockSpec(memory_space=pltpu.SMEM),
        ],
        out_specs=(
            pl.BlockSpec(memory_space=pl.ANY),
            pl.BlockSpec(memory_space=pl.ANY),
        ),
        scratch_shapes=[
            pltpu.VMEM((order, order), bf16),
            pltpu.VMEM((face, cases), f32),
            pltpu.VMEM((2, rows, cases), f32),
            pltpu.VMEM((2, rows, cases), bf16),
            pltpu.VMEM((2, rows, cases), bf16),
            pltpu.VMEM((1, face), jnp.int32),
            pltpu.VMEM((2, face), jnp.int32),
            pltpu.VMEM((2, face), jnp.int32),
            pltpu.VMEM((face, cases), f32),
            pltpu.VMEM((2, face, cases), f32),
            pltpu.VMEM((2, face, cases), f32),
            pltpu.VMEM((2, face, cases), f32),
            pltpu.VMEM((2, order, cases), bf16),
            pltpu.VMEM((2, face, cases), f32),
            pltpu.VMEM((ITERS, 2, face, cases), bf16),
            pltpu.VMEM((ITERS, 2, rows, cases), bf16),
            pltpu.VMEM((ITERS, 2, rows // 2, cases), bf16),
            pltpu.VMEM((ITERS, 2, rows // 2, cases), bf16),
            pltpu.VMEM((ITERS, 2, rows, cases), bf16),
            pltpu.VMEM((ITERS, 2, 2, cases), f32),
            pltpu.VMEM((ITERS, 2, n, 2, cases), f32),
            pltpu.SemaphoreType.DMA((3,)),
            pltpu.SemaphoreType.DMA((2,)),
            pltpu.SemaphoreType.DMA((3,)),
            pltpu.SemaphoreType.DMA((3,)),
            pltpu.SemaphoreType.DMA((ITERS, 2)),
            pltpu.SemaphoreType.DMA((ITERS, 2)),
            pltpu.SemaphoreType.DMA((ITERS, 2, 3)),
            pltpu.SemaphoreType.DMA((ITERS, 2, 3)),
            pltpu.SemaphoreType.DMA((ITERS, 2, n)),
            pltpu.SemaphoreType.DMA((ITERS, 2, n)),
        ],
        compiler_params=pltpu.CompilerParams(
            collective_id=0,
            has_side_effects=True,
            vmem_limit_bytes=52 * 1024 * 1024,
        ),
        cost_estimate=pl.CostEstimate(
            flops=2 * ITERS * order * order * cases,
            bytes_accessed=2 * order * order + 12 * face * cases,
            transcendentals=0,
        ),
    )(*inputs, costs)


def solution(mesh):
    return jax.shard_map(
        on_device,
        mesh=mesh,
        in_specs=(
            P("lend", "wide", None, None),
            P("lend", "wide", None),
            P("lend", "wide"),
            P("lend", "wide"),
        ),
        out_specs=(P("lend", "wide", None), P("lend", "wide", None)),
        check_vma=False,
    )
```

```python
import functools

import jax
import jax.numpy as jnp
from jax import lax
from jax.experimental import pallas as pl
from jax.experimental.pallas import tpu as pltpu
from jax.sharding import PartitionSpec as P

ROWBLK = 128
ITERS = 4
RIDGE = 1.0
FIRST_STEP = 0.1
EPSILON = 1e-06
PARTS = 2
MESH = pl.DeviceIdType.MESH


def kernel(
    n,
    op_hbm,
    rhs_hbm,
    contact_hbm,
    costs_ref,
    lam_hbm,
    grad_hbm,
    op,
    rhs,
    own_rhs,
    rhs_send,
    rhs_recv,
    contact,
    contact_recv,
    floor,
    lam,
    grad,
    field,
    operand,
    out,
    y_send,
    top_recv,
    low_recv,
    part_send,
    part_recv,
    load_sem,
    out_sem,
    first_send_sem,
    first_recv_sem,
    y_send_sem,
    y_recv_sem,
    part_send_sem,
    part_recv_sem,
):
    order = op.shape[0]
    face, cases = rhs.shape
    rows = face // PARTS
    me = lax.axis_index("wide")
    right = {"wide": lax.rem(me + 1, n)}
    left = {"wide": lax.rem(me + n - 1, n)}
    sent = []

    def send(src, dst, send_sem, recv_sem, where, at_once=True):
        copy = pltpu.make_async_remote_copy(
            src_ref=src,
            dst_ref=dst,
            send_sem=send_sem,
            recv_sem=recv_sem,
            device_id=where,
            device_id_type=MESH,
        )
        if at_once:
            copy.start()
        sent.append(copy)
        return copy

    load_rhs = pltpu.make_async_copy(rhs_hbm.at[0], rhs, load_sem.at[0])
    load_rhs.start()
    load_contact = pltpu.make_async_copy(contact_hbm, contact, load_sem.at[1])
    load_contact.start()
    load_op = pltpu.make_async_copy(op_hbm.at[0, 0], op, load_sem.at[2])
    load_op.start()

    barrier = pltpu.get_barrier_semaphore()
    for d in range(1, n):
        pl.semaphore_signal(
            barrier, inc=1, device_id={"wide": lax.rem(me + d, n)}, device_id_type=MESH
        )

    def first_lanes(count):
        return lax.broadcasted_iota(jnp.int32, (count, cases), 1) < cases // 2

    def swap(values):
        return pltpu.roll(values, cases // 2, axis=1)

    def active(start, count):
        row = lax.broadcasted_iota(jnp.int32, (count, cases), 0) + start
        return jnp.where(first_lanes(count), row, row + rows) < live

    def exchange(upper, lower, half):
        first = first_lanes(upper.shape[0])
        if half == 0:
            return jnp.where(first, upper, swap(lower))
        return jnp.where(first, swap(upper), lower)

    def make_floor(flags, base):
        for start in range(0, rows, ROWBLK):
            both = [
                jnp.broadcast_to(
                    jnp.where(flags[0:1, at : at + ROWBLK] == 1, 0.0, -jnp.inf).astype(
                        jnp.float32
                    ),
                    (cases // 2, ROWBLK),
                )
                for at in (start, start + rows)
            ]
            floor[base + start : base + start + ROWBLK, :] = jnp.concatenate(
                both, axis=0
            ).T

    load_rhs.wait()
    for half in range(2):
        packed = exchange(rhs[0:rows, :], rhs[rows:face, :], half)
        own_rhs[half] = packed
        rhs_send[half] = packed.astype(jnp.bfloat16)
    load_contact.wait()
    live = costs_ref[0, 0] * ROWBLK

    pl.semaphore_wait(barrier, n - 1)

    first = [
        send(
            rhs_send.at[half],
            rhs_recv.at[half],
            first_send_sem.at[half],
            first_recv_sem.at[half],
            right,
        )
        for half in range(2)
    ]
    facts = send(contact, contact_recv, first_send_sem.at[2], first_recv_sem.at[2], right)

    def advance(half, own, steplen, gradient_at, begins):
        base = rows if own else 0
        squares = jnp.zeros((8, cases), jnp.float32)
        for here in range(0, rows, ROWBLK):
            at = slice(base + here, base + here + ROWBLK)
            g = gradient_at(here)
            before = jnp.zeros_like(g) if begins else lam[half, at, :]
            moved = jnp.maximum(before - steplen * g, floor[at, :])
            change = moved - before
            lam[half, at, :] = moved
            grad[half, at, :] = g + RIDGE * change
            if own:
                squares += jnp.sum(
                    (change * change).reshape(ROWBLK // 8, 8, cases), axis=0
                )
            masked = jnp.where(
                active(2 * base + here, ROWBLK), change if own else -change, 0.0
            )
            field[half, at, :] = masked
            turned = swap(masked)
            lanes = first_lanes(ROWBLK)
            slot = 2 * base + here
            operand[half, slot : slot + ROWBLK, :] = jnp.where(
                lanes, masked, turned
            ).astype(jnp.bfloat16)
            operand[half, slot + rows : slot + rows + ROWBLK, :] = jnp.where(
                lanes, turned, masked
            ).astype(jnp.bfloat16)
        return squares

    def fold(sums):
        total = jnp.sum(sums, axis=0, keepdims=True)
        return total + swap(total)

    steplen = [jnp.full((1, cases), FIRST_STEP, jnp.float32)] * 2
    make_floor(contact, rows)
    squares = [
        advance(
            half,
            True,
            steplen[half],
            lambda i, half=half: -own_rhs[half, i : i + ROWBLK, :],
            True,
        )
        for half in range(2)
    ]
    facts.wait_recv()
    make_floor(contact_recv, 0)
    tops, lows, parts, sums = [None] * 2, [None] * 2, [None] * 2, [None] * 2
    for it in range(ITERS):
        finished = it + 1 == ITERS
        for half in range(2):
            if it == 0:
                first[half].wait_recv()
                advance(
                    half,
                    False,
                    steplen[half],
                    lambda i: -rhs_recv[half, i : i + ROWBLK, :].astype(jnp.float32),
                    True,
                )
            else:
                total = sums[half]
                for copy in parts[half]:
                    copy.wait_recv()
                for d in range(1, n):
                    total = total + part_recv[it - 1, half, d]
                steplen[half] = (total[0:1] + EPSILON) / (total[1:2] + EPSILON)

                def own_gradient(i):
                    came = top_recv[it - 1, half, i : i + ROWBLK, :]
                    at = slice(rows + i, rows + i + ROWBLK)
                    return grad[half, at, :] - came.astype(jnp.float32)

                def left_gradient(i):
                    came = low_recv[it - 1, half, i : i + ROWBLK, :]
                    at = slice(i, i + ROWBLK)
                    return grad[half, at, :] + came.astype(jnp.float32)

                tops[half].wait_recv()
                squares[half] = advance(half, True, steplen[half], own_gradient, False)
                lows[half].wait_recv()
                advance(half, False, steplen[half], left_gradient, False)
            if it == 0 and half == 0:
                load_op.wait()

            bending = RIDGE * squares[half]
            for base in (0, rows):
                y = jnp.dot(
                    op[2 * base : 2 * base + face, :],
                    operand[half],
                    preferred_element_type=jnp.float32,
                )
                y = jnp.where(first_lanes(rows), y[0:rows, :], y[rows:face, :])
                y = jnp.where(active(2 * base, rows), y, 0.0)
                at = slice(base, base + rows)
                if not finished or base == 0:
                    y_send[it, half, at, :] = y.astype(jnp.bfloat16)
                if base == 0:
                    tops[half] = send(
                        y_send.at[it, half, pl.ds(0, rows)],
                        top_recv.at[it, half],
                        y_send_sem.at[it, half, 0],
                        y_recv_sem.at[it, half, 0],
                        left,
                        finished,
                    )
                    if not finished:
                        grad[half, at, :] = grad[half, at, :] - y
                else:
                    grad[half, at, :] = grad[half, at, :] + y
                if not finished:
                    bending += jnp.sum(
                        (field[half, at, :] * y).reshape(rows // 8, 8, cases), axis=0
                    )
            if finished:
                continue
            sums[half] = jnp.concatenate([fold(squares[half]), fold(bending)], axis=0)
            part_send[it, half] = sums[half]
            parts[half] = []
            for d in range(1, n):
                parts[half].append(
                    send(
                        part_send.at[it, half],
                        part_recv.at[it, half, d],
                        part_send_sem.at[it, half, d],
                        part_recv_sem.at[it, half, d],
                        {"wide": lax.rem(me + d, n)},
                    )
                )
            tops[half].start()
            lows[half] = send(
                y_send.at[it, half, pl.ds(rows, rows)],
                low_recv.at[it, half],
                y_send_sem.at[it, half, 1],
                y_recv_sem.at[it, half, 1],
                right,
            )

    def unpack(source):
        return [
            exchange(source[0, rows:face, :], source[1, rows:face, :], part)
            for part in range(2)
        ]

    saves = []

    def save(number, values, target):
        for part in range(2):
            out[number, part * rows : (part + 1) * rows, :] = values[part]
        copy = pltpu.make_async_copy(out.at[number], target.at[0], out_sem.at[number])
        copy.start()
        saves.append(copy)

    save(0, unpack(lam), lam_hbm)
    for half in range(2):
        tops[half].wait_recv()
        came = top_recv[ITERS - 1, half].astype(jnp.float32)
        grad[half, rows:face, :] = grad[half, rows:face, :] - came
    save(1, unpack(grad), grad_hbm)
    for copy in sent:
        copy.wait_send()
    for copy in saves:
        copy.wait()


def on_device(operators, dual_rhs, contact, costs):
    n = lax.axis_size("wide")
    order = operators.shape[2]
    face, cases = dual_rhs.shape[1:]
    rows = face // PARTS
    f32, bf16 = jnp.float32, jnp.bfloat16
    shape = jax.ShapeDtypeStruct(dual_rhs.shape, f32)
    inputs = [
        pltpu.with_memory_space_constraint(x, pltpu.HBM)
        for x in (operators, dual_rhs, contact)
    ]
    return pl.pallas_call(
        functools.partial(kernel, n),
        out_shape=(shape, shape),
        in_specs=[
            pl.BlockSpec(memory_space=pl.ANY),
            pl.BlockSpec(memory_space=pl.ANY),
            pl.BlockSpec(memory_space=pl.ANY),
            pl.BlockSpec(memory_space=pltpu.SMEM),
        ],
        out_specs=(
            pl.BlockSpec(memory_space=pl.ANY),
            pl.BlockSpec(memory_space=pl.ANY),
        ),
        scratch_shapes=[
            pltpu.VMEM((order, order), bf16),
            pltpu.VMEM((face, cases), f32),
            pltpu.VMEM((2, rows, cases), f32),
            pltpu.VMEM((2, rows, cases), bf16),
            pltpu.VMEM((2, rows, cases), bf16),
            pltpu.VMEM((1, face), jnp.int32),
            pltpu.VMEM((1, face), jnp.int32),
            pltpu.VMEM((face, cases), f32),
            pltpu.VMEM((2, face, cases), f32),
            pltpu.VMEM((2, face, cases), f32),
            pltpu.VMEM((2, face, cases), f32),
            pltpu.VMEM((2, order, cases), bf16),
            pltpu.VMEM((2, face, cases), f32),
            pltpu.VMEM((ITERS, 2, face, cases), bf16),
            pltpu.VMEM((ITERS, 2, rows, cases), bf16),
            pltpu.VMEM((ITERS, 2, rows, cases), bf16),
            pltpu.VMEM((ITERS, 2, 2, cases), f32),
            pltpu.VMEM((ITERS, 2, n, 2, cases), f32),
            pltpu.SemaphoreType.DMA((3,)),
            pltpu.SemaphoreType.DMA((2,)),
            pltpu.SemaphoreType.DMA((3,)),
            pltpu.SemaphoreType.DMA((3,)),
            pltpu.SemaphoreType.DMA((ITERS, 2, 2)),
            pltpu.SemaphoreType.DMA((ITERS, 2, 2)),
            pltpu.SemaphoreType.DMA((ITERS, 2, n)),
            pltpu.SemaphoreType.DMA((ITERS, 2, n)),
        ],
        compiler_params=pltpu.CompilerParams(
            collective_id=0,
            has_side_effects=True,
            vmem_limit_bytes=52 * 1024 * 1024,
        ),
        cost_estimate=pl.CostEstimate(
            flops=2 * ITERS * order * order * cases,
            bytes_accessed=2 * order * order + 12 * face * cases,
            transcendentals=0,
        ),
    )(*inputs, costs)


def solution(mesh):
    return jax.shard_map(
        on_device,
        mesh=mesh,
        in_specs=(
            P("lend", "wide", None, None),
            P("lend", "wide", None),
            P("lend", "wide"),
            P("lend", "wide"),
        ),
        out_specs=(P("lend", "wide", None), P("lend", "wide", None)),
        check_vma=False,
    )
```

```python
import functools

import jax
import jax.numpy as jnp
from jax import lax
from jax.experimental import pallas as pl
from jax.experimental.pallas import tpu as pltpu
from jax.sharding import PartitionSpec as P

ROWBLK = 128
ITERS = 4
RIDGE = 1.0
FIRST_STEP = 0.1
EPSILON = 1e-06
PARTS = 2
MESH = pl.DeviceIdType.MESH


def kernel(
    n,
    op_hbm,
    rhs_hbm,
    contact_hbm,
    costs_ref,
    lam_hbm,
    grad_hbm,
    op,
    rhs,
    own_rhs,
    rhs_send,
    rhs_recv,
    contact,
    facts_send,
    facts_recv,
    floor,
    lam,
    grad,
    field,
    operand,
    out,
    y_send,
    top_recv,
    pair_recv,
    low_send,
    low_recv,
    part_send,
    part_recv,
    load_sem,
    out_sem,
    first_send_sem,
    first_recv_sem,
    y_send_sem,
    y_recv_sem,
    low_send_sem,
    low_recv_sem,
    part_send_sem,
    part_recv_sem,
):
    order = op.shape[0]
    face, cases = rhs.shape
    rows = face // PARTS
    me = lax.axis_index("wide")
    right = {"wide": lax.rem(me + 1, n)}
    left = {"wide": lax.rem(me + n - 1, n)}
    lend = lax.axis_index("lend")
    side = lax.rem(lend, 2)
    pair = {"lend": lend + 1 - 2 * side}
    share = rows // 2
    mine = pl.multiple_of(side * share, share)
    theirs = pl.multiple_of((1 - side) * share, share)
    sent = []

    def send(src, dst, send_sem, recv_sem, where, at_once=True):
        copy = pltpu.make_async_remote_copy(
            src_ref=src,
            dst_ref=dst,
            send_sem=send_sem,
            recv_sem=recv_sem,
            device_id=where,
            device_id_type=MESH,
        )
        if at_once:
            copy.start()
        sent.append(copy)
        return copy

    load_rhs = pltpu.make_async_copy(rhs_hbm.at[0], rhs, load_sem.at[0])
    load_rhs.start()
    load_contact = pltpu.make_async_copy(contact_hbm, contact, load_sem.at[1])
    load_contact.start()
    load_op = pltpu.make_async_copy(op_hbm.at[0, 0], op, load_sem.at[2])
    load_op.start()

    barrier = pltpu.get_barrier_semaphore()
    for d in range(1, n):
        pl.semaphore_signal(
            barrier, inc=1, device_id={"wide": lax.rem(me + d, n)}, device_id_type=MESH
        )

    pl.semaphore_signal(barrier, inc=1, device_id=pair, device_id_type=MESH)

    def first_lanes(count):
        return lax.broadcasted_iota(jnp.int32, (count, cases), 1) < cases // 2

    def swap(values):
        return pltpu.roll(values, cases // 2, axis=1)

    def active(start, count, bound):
        row = lax.broadcasted_iota(jnp.int32, (count, cases), 0) + start
        return jnp.where(first_lanes(count), row, row + rows) < bound

    def exchange(upper, lower, half):
        first = first_lanes(upper.shape[0])
        if half == 0:
            return jnp.where(first, upper, swap(lower))
        return jnp.where(first, swap(upper), lower)

    def make_floor(flags, base):
        for start in range(0, rows, ROWBLK):
            both = [
                jnp.broadcast_to(
                    jnp.where(flags[0:1, at : at + ROWBLK] == 1, 0.0, -jnp.inf).astype(
                        jnp.float32
                    ),
                    (cases // 2, ROWBLK),
                )
                for at in (start, start + rows)
            ]
            floor[base + start : base + start + ROWBLK, :] = jnp.concatenate(
                both, axis=0
            ).T

    load_rhs.wait()
    for half in range(2):
        packed = exchange(rhs[0:rows, :], rhs[rows:face, :], half)
        own_rhs[half] = packed
        rhs_send[half] = packed.astype(jnp.bfloat16)
    load_contact.wait()
    live = costs_ref[0, 0] * ROWBLK
    facts_send[0:1, :] = contact[...]
    facts_send[1:2, :] = jnp.full((1, face), live, jnp.int32)

    pl.semaphore_wait(barrier, n)

    first = [
        send(
            rhs_send.at[half],
            rhs_recv.at[half],
            first_send_sem.at[half],
            first_recv_sem.at[half],
            right,
        )
        for half in range(2)
    ]
    facts = send(facts_send, facts_recv, first_send_sem.at[2], first_recv_sem.at[2], right)

    def advance(half, own, steplen, gradient_at, begins):
        base = rows if own else 0
        squares = jnp.zeros((8, cases), jnp.float32)
        for here in range(0, rows, ROWBLK):
            at = slice(base + here, base + here + ROWBLK)
            g = gradient_at(here)
            before = jnp.zeros_like(g) if begins else lam[half, at, :]
            moved = jnp.maximum(before - steplen * g, floor[at, :])
            change = moved - before
            lam[half, at, :] = moved
            grad[half, at, :] = g + RIDGE * change
            if own:
                squares += jnp.sum(
                    (change * change).reshape(ROWBLK // 8, 8, cases), axis=0
                )
            masked = jnp.where(
                active(2 * base + here, ROWBLK, live), change if own else -change, 0.0
            )
            field[half, at, :] = masked
            turned = swap(masked)
            lanes = first_lanes(ROWBLK)
            slot = 2 * base + here
            operand[half, slot : slot + ROWBLK, :] = jnp.where(
                lanes, masked, turned
            ).astype(jnp.bfloat16)
            operand[half, slot + rows : slot + rows + ROWBLK, :] = jnp.where(
                lanes, turned, masked
            ).astype(jnp.bfloat16)
        return squares

    def fold(sums):
        total = jnp.sum(sums, axis=0, keepdims=True)
        return total + swap(total)

    steplen = [jnp.full((1, cases), FIRST_STEP, jnp.float32)] * 2
    make_floor(contact, rows)
    squares = [
        advance(
            half,
            True,
            steplen[half],
            lambda i, half=half: -own_rhs[half, i : i + ROWBLK, :],
            True,
        )
        for half in range(2)
    ]
    facts.wait_recv()
    make_floor(facts_recv, 0)
    live_left = facts_recv[1:2, 0:cases]
    tops, swaps, lows = [None] * 2, [None] * 2, [None] * 2
    parts, sums = [None] * 2, [None] * 2
    for it in range(ITERS):
        finished = it + 1 == ITERS
        for half in range(2):
            if it == 0:
                first[half].wait_recv()
                advance(
                    half,
                    False,
                    steplen[half],
                    lambda i: -rhs_recv[half, i : i + ROWBLK, :].astype(jnp.float32),
                    True,
                )
            else:
                lows[half].wait_recv()
                forward = send(
                    low_recv.at[it - 1, half, pl.ds(mine, share)],
                    low_recv.at[it - 1, half, pl.ds(mine, share)],
                    low_send_sem.at[it - 1, half, 2],
                    low_recv_sem.at[it - 1, half, 2],
                    pair,
                )
                total = sums[half]
                for copy in parts[half]:
                    copy.wait_recv()
                for d in range(1, n):
                    total = total + part_recv[it - 1, half, d]
                steplen[half] = (total[0:1] + EPSILON) / (total[1:2] + EPSILON)

                def own_gradient(i):
                    came = top_recv[it - 1, half, i : i + ROWBLK, :]
                    at = slice(rows + i, rows + i + ROWBLK)
                    return grad[half, at, :] - came.astype(jnp.float32)

                def left_gradient(i):
                    came = low_recv[it - 1, half, i : i + ROWBLK, :].astype(jnp.float32)
                    ours = active(face + i, ROWBLK, live_left)
                    at = slice(i, i + ROWBLK)
                    return grad[half, at, :] + jnp.where(ours, came, 0.0)

                tops[half].wait_recv()
                squares[half] = advance(half, True, steplen[half], own_gradient, False)
                forward.wait_recv()
                advance(half, False, steplen[half], left_gradient, False)
            if it == 0 and half == 0:
                load_op.wait()

            bending = RIDGE * squares[half]
            for base in (0, rows) if finished else (rows, 0):
                y = jnp.dot(
                    op[2 * base : 2 * base + face, :],
                    operand[half],
                    preferred_element_type=jnp.float32,
                )
                y = jnp.where(first_lanes(rows), y[0:rows, :], y[rows:face, :])
                y = jnp.where(active(2 * base, rows, live), y, 0.0)
                at = slice(base, base + rows)
                if not finished or base == 0:
                    y_send[it, half, at, :] = y.astype(jnp.bfloat16)
                if base == 0:
                    tops[half] = send(
                        y_send.at[it, half, pl.ds(0, rows)],
                        top_recv.at[it, half],
                        y_send_sem.at[it, half],
                        y_recv_sem.at[it, half],
                        left,
                        finished,
                    )
                    if not finished:
                        grad[half, at, :] = grad[half, at, :] - y
                else:
                    if not finished:
                        swaps[half] = send(
                            y_send.at[it, half, pl.ds(rows + theirs, share)],
                            pair_recv.at[it, half],
                            low_send_sem.at[it, half, 0],
                            low_recv_sem.at[it, half, 0],
                            pair,
                        )
                    grad[half, at, :] = grad[half, at, :] + y
                if not finished:
                    bending += jnp.sum(
                        (field[half, at, :] * y).reshape(rows // 8, 8, cases), axis=0
                    )
            if finished:
                continue
            sums[half] = jnp.concatenate([fold(squares[half]), fold(bending)], axis=0)
            part_send[it, half] = sums[half]
            parts[half] = []
            for d in sorted(range(1, n), key=lambda d: -min(d, n - d)):
                parts[half].append(
                    send(
                        part_send.at[it, half],
                        part_recv.at[it, half, d],
                        part_send_sem.at[it, half, d],
                        part_recv_sem.at[it, half, d],
                        {"wide": lax.rem(me + d, n)},
                    )
                )
            tops[half].start()
            swaps[half].wait_recv()
            low_send[it, half] = (
                y_send[it, half, pl.ds(rows + mine, share), :] + pair_recv[it, half]
            )
            lows[half] = send(
                low_send.at[it, half],
                low_recv.at[it, half, pl.ds(mine, share)],
                low_send_sem.at[it, half, 1],
                low_recv_sem.at[it, half, 1],
                right,
            )

    def unpack(source):
        return [
            exchange(source[0, rows:face, :], source[1, rows:face, :], part)
            for part in range(2)
        ]

    saves = []

    def save(number, values, target):
        for part in range(2):
            out[number, part * rows : (part + 1) * rows, :] = values[part]
        copy = pltpu.make_async_copy(out.at[number], target.at[0], out_sem.at[number])
        copy.start()
        saves.append(copy)

    save(0, unpack(lam), lam_hbm)
    for half in range(2):
        tops[half].wait_recv()
        came = top_recv[ITERS - 1, half].astype(jnp.float32)
        grad[half, rows:face, :] = grad[half, rows:face, :] - came
    save(1, unpack(grad), grad_hbm)
    for copy in sent:
        copy.wait_send()
    for copy in saves:
        copy.wait()


def on_device(operators, dual_rhs, contact, costs):
    n = lax.axis_size("wide")
    order = operators.shape[2]
    face, cases = dual_rhs.shape[1:]
    rows = face // PARTS
    f32, bf16 = jnp.float32, jnp.bfloat16
    shape = jax.ShapeDtypeStruct(dual_rhs.shape, f32)
    inputs = [
        pltpu.with_memory_space_constraint(x, pltpu.HBM)
        for x in (operators, dual_rhs, contact)
    ]
    return pl.pallas_call(
        functools.partial(kernel, n),
        out_shape=(shape, shape),
        in_specs=[
            pl.BlockSpec(memory_space=pl.ANY),
            pl.BlockSpec(memory_space=pl.ANY),
            pl.BlockSpec(memory_space=pl.ANY),
            pl.BlockSpec(memory_space=pltpu.SMEM),
        ],
        out_specs=(
            pl.BlockSpec(memory_space=pl.ANY),
            pl.BlockSpec(memory_space=pl.ANY),
        ),
        scratch_shapes=[
            pltpu.VMEM((order, order), bf16),
            pltpu.VMEM((face, cases), f32),
            pltpu.VMEM((2, rows, cases), f32),
            pltpu.VMEM((2, rows, cases), bf16),
            pltpu.VMEM((2, rows, cases), bf16),
            pltpu.VMEM((1, face), jnp.int32),
            pltpu.VMEM((2, face), jnp.int32),
            pltpu.VMEM((2, face), jnp.int32),
            pltpu.VMEM((face, cases), f32),
            pltpu.VMEM((2, face, cases), f32),
            pltpu.VMEM((2, face, cases), f32),
            pltpu.VMEM((2, face, cases), f32),
            pltpu.VMEM((2, order, cases), bf16),
            pltpu.VMEM((2, face, cases), f32),
            pltpu.VMEM((ITERS, 2, face, cases), bf16),
            pltpu.VMEM((ITERS, 2, rows, cases), bf16),
            pltpu.VMEM((ITERS, 2, rows // 2, cases), bf16),
            pltpu.VMEM((ITERS, 2, rows // 2, cases), bf16),
            pltpu.VMEM((ITERS, 2, rows, cases), bf16),
            pltpu.VMEM((ITERS, 2, 2, cases), f32),
            pltpu.VMEM((ITERS, 2, n, 2, cases), f32),
            pltpu.SemaphoreType.DMA((3,)),
            pltpu.SemaphoreType.DMA((2,)),
            pltpu.SemaphoreType.DMA((3,)),
            pltpu.SemaphoreType.DMA((3,)),
            pltpu.SemaphoreType.DMA((ITERS, 2)),
            pltpu.SemaphoreType.DMA((ITERS, 2)),
            pltpu.SemaphoreType.DMA((ITERS, 2, 3)),
            pltpu.SemaphoreType.DMA((ITERS, 2, 3)),
            pltpu.SemaphoreType.DMA((ITERS, 2, n)),
            pltpu.SemaphoreType.DMA((ITERS, 2, n)),
        ],
        compiler_params=pltpu.CompilerParams(
            collective_id=0,
            has_side_effects=True,
            vmem_limit_bytes=52 * 1024 * 1024,
        ),
        cost_estimate=pl.CostEstimate(
            flops=2 * ITERS * order * order * cases,
            bytes_accessed=2 * order * order + 12 * face * cases,
            transcendentals=0,
        ),
    )(*inputs, costs)


def solution(mesh):
    return jax.shard_map(
        on_device,
        mesh=mesh,
        in_specs=(
            P("lend", "wide", None, None),
            P("lend", "wide", None),
            P("lend", "wide"),
            P("lend", "wide"),
        ),
        out_specs=(P("lend", "wide", None), P("lend", "wide", None)),
        check_vma=False,
    )
```
